32 devices in a mesh: pos: 4 (over y, core), stream: 8 (over z, x).
Axes of the slice: x: 2, y: 2, z: 4, core: 2. Of those that a mesh axis runs over, the one named last changes fastest.
Arguments:
- tokens_in: bfloat16 [8, 2048, 8192], P('stream', 'pos'), may hold values from -6 to 6
- proj_in: bfloat16 [8, 2048, 256], P('stream', 'pos'), may hold values from -1.75 to 1.75
- step_raw: bfloat16 [8, 2048, 128], P('stream', 'pos')
- decay_log: float32 [128], replicated, may hold values from -0.7 to 0.7
- head_skip_weight: float32 [128], replicated, may hold values from 0.5 to 1.5
- row_counts: int32 [4, 8, 8], replicated, may hold values from 32 to 96, as said below
Outputs:
- layer_out: bfloat16 [8, 2048, 8192], P('stream', 'pos')
The draws below stay inside these ranges and needn't reach their ends.
Inputs may be any that keep to these rules, and one draw needn't show every extreme that they name: For each p, every row and every column of row_counts[p] sums to 512; all rows and columns of row_counts[p] hold the same list of values in some order, and the list splits into pairs whose sum is twice the list's mean; each row_counts[p] holds the value 96.
All inputs are finite; a program needn't handle non-finite values.
Results may differ from the reference program's by a relative error of at most 0.0037.
Values may be sent and summed in bfloat16 or wider, within the bound.
A program may use at most 256 MiB of HBM per device.

```python
from functools import partial
import jax
import jax.numpy as jnp
from jax import lax

HEADS = 128
HDIM = 64
STATE = 128
TOK_DEV = 512
BLOCK = 512
INNER = 8192
SEQUENCE_SLOTS = 2048
N_POS = 4
N_STREAM = 8


def head_law(key):
    law_key = jax.random.fold_in(key, 7071)
    derived_prng_keys = jax.random.split(law_key, 3)
    fast_share = 0.5
    fast_heads = jax.random.uniform(derived_prng_keys[0], (HEADS,)) < fast_share
    absolute_amplitude = jnp.exp(jax.random.uniform(derived_prng_keys[1], (HEADS,), minval=-0.69, maxval=0.69))
    spread = jax.random.uniform(derived_prng_keys[2], (HEADS,))
    per_step = jnp.where(fast_heads, 1.0 / (10.0 + 30.0 * spread), (0.5 + spread) / SEQUENCE_SLOTS)
    return (absolute_amplitude, per_step)


def draw_decay_log(key, part):
    absolute_amplitude, per_step = head_law(key)
    return jnp.log(absolute_amplitude)


def draw_step_raw(key, part):
    absolute_amplitude, per_step = head_law(key)
    derived_prng_keys = jax.random.split(jax.random.fold_in(key, 313), 3)
    jitter = jnp.clip(0.3 * jax.random.normal(derived_prng_keys[0], (N_STREAM, SEQUENCE_SLOTS, HEADS)), -0.45, 0.45)
    discretization_deltas = (per_step / absolute_amplitude)[None, None, :] * jnp.exp(jitter)
    arrival_bundles = jax.random.uniform(derived_prng_keys[1], (N_STREAM, SEQUENCE_SLOTS, 1)) < 3.0 / SEQUENCE_SLOTS
    excitation_level = jax.random.uniform(derived_prng_keys[2], (N_STREAM, SEQUENCE_SLOTS, HEADS), minval=0.22, maxval=0.69)
    discretization_deltas = jnp.where(arrival_bundles, excitation_level / absolute_amplitude[None, None, :], discretization_deltas)
    return jnp.log(jnp.expm1(discretization_deltas)).astype(jnp.bfloat16)


def draw_row_counts(key, part):
    base_count = TOK_DEV // N_STREAM
    half_base = base_count // 2
    pair_count = N_STREAM // 2

    def one_place(place_key):
        derived_prng_keys = jax.random.split(place_key, 4)
        shift_size = jax.random.randint(derived_prng_keys[0], (pair_count,), 0, half_base + 1)
        shift_size = jnp.where(jnp.arange(pair_count) == 0, half_base, shift_size)
        values = jnp.concatenate([base_count + shift_size, base_count - shift_size])
        reorder = jax.random.permutation(derived_prng_keys[1], N_STREAM)
        values = jnp.take(values, reorder)
        row_perm = jax.random.permutation(derived_prng_keys[2], N_STREAM)
        col_perm = jax.random.permutation(derived_prng_keys[3], N_STREAM)
        offset = (col_perm[None, :] - row_perm[:, None]) % N_STREAM
        return jnp.take(values, offset).astype(jnp.int32)
    return jax.vmap(one_place)(jax.random.split(jax.random.fold_in(key, 977), N_POS))


def levels(stream_key, shape, shards, low, top_value):
    gain = 1.0
    for axis_at, blocks in shards:
        heights = jax.random.uniform(jax.random.fold_in(jax.random.fold_in(stream_key, 6), axis_at), (blocks,), jnp.float32, low / len(shards), top_value / len(shards))
        gain = gain * jnp.repeat(jnp.exp(heights), shape[axis_at] // blocks).reshape((-1,) + (1,) * (len(shape) - 1 - axis_at))
    return gain


def gaussian(key, extent, scale, most, shards=(), kind=jnp.bfloat16):
    array = scale * jax.random.normal(key, extent, jnp.float32)
    if shards:
        array = array * levels(key, extent, shards, -0.22, 0.18)
    return jnp.clip(array, -most, most).astype(kind)


def setup_inputs(seed: int = 0) -> dict:
    streams_of = jax.random.split(jax.random.key(seed), 7)
    tokens_in = gaussian(streams_of[0], (N_STREAM, SEQUENCE_SLOTS, INNER), 1.0, 6.0, ((0, 8), (1, 4)))
    proj_in = gaussian(streams_of[1], (N_STREAM, SEQUENCE_SLOTS, 2 * STATE), (STATE ** -0.25), 1.75, ((0, 8), (1, 4)))
    step_raw = draw_step_raw(jax.random.fold_in(streams_of[6], 71), 0)
    decay_log = draw_decay_log(jax.random.fold_in(streams_of[6], 71), 0)
    head_skip_weight = jnp.clip(jax.random.uniform(streams_of[4], (HEADS,), jnp.float32, 0.5, 1.5), 0.5, 1.5)
    row_counts = draw_row_counts(jax.random.fold_in(streams_of[6], 71), 0)
    return {"tokens_in": tokens_in, "proj_in": proj_in, "step_raw": step_raw, "decay_log": decay_log, "head_skip_weight": head_skip_weight, "row_counts": row_counts}


def stream_blocks(carry_state, block_data, decay_rates, head_skip_weight):
    tokens, input_projections, steps_raw = block_data
    length = tokens.shape[0]
    token_heads = tokens.reshape(length, HEADS, HDIM).astype(jnp.float32)
    inputs = input_projections[:, :STATE]
    readout = input_projections[:, STATE:]
    discretization_deltas = jax.nn.softplus(steps_raw.astype(jnp.float32))
    cumulated = jnp.cumsum(discretization_deltas * decay_rates[None, :], axis=0)
    scores = jnp.dot(readout, inputs.T, preferred_element_type=jnp.float32)
    causal = jnp.arange(length, dtype=jnp.int32)[:, None] >= jnp.arange(length, dtype=jnp.int32)[None, :]
    log_decay = jnp.where(causal[:, :, None], cumulated[:, None, :] - cumulated[None, :, :], -jnp.inf)
    weights = (scores[:, :, None] * jnp.exp(log_decay) * discretization_deltas[None, :, :]).astype(jnp.bfloat16)
    weights = lax.optimization_barrier(weights).astype(jnp.float32)
    local_part = jnp.einsum("tsh,shp->thp", weights, token_heads)
    readable = lax.optimization_barrier(carry_state.astype(jnp.bfloat16)).astype(jnp.float32)
    inherited = jnp.einsum("tn,hnp->thp", readout.astype(jnp.float32), readable)
    total = local_part + jnp.exp(cumulated)[:, :, None] * inherited + head_skip_weight[None, :, None] * token_heads
    ending = cumulated[-1]
    scaled = ((jnp.exp(ending[None, :] - cumulated) * discretization_deltas)[:, :, None] * token_heads).astype(jnp.bfloat16)
    scaled = lax.optimization_barrier(scaled).astype(jnp.float32)
    carried = jnp.einsum("sn,shp->hnp", inputs.astype(jnp.float32), scaled)
    new_state = jnp.exp(ending)[:, None, None] * carry_state + carried
    return new_state, total.astype(jnp.bfloat16).reshape(length, HEADS * HDIM)


def reference(tokens_in, proj_in, step_raw, decay_log, head_skip_weight, row_counts):
    decay_rates = -jnp.exp(decay_log)
    send_start = (jnp.cumsum(row_counts, axis=2) - row_counts).astype(jnp.int32)
    recv_end = jnp.cumsum(row_counts, axis=1).astype(jnp.int32)
    recv_start = (recv_end - row_counts).astype(jnp.int32)
    positions = jnp.arange(TOK_DEV, dtype=jnp.int32)
    source = jnp.sum((recv_end[:, :, :, None] <= positions[None, None, None, :]).astype(jnp.int32), axis=1).astype(jnp.int32)
    recv_from = jnp.take_along_axis(jnp.transpose(recv_start, (0, 2, 1)), source, axis=2)
    outgoing_offsets = jnp.take_along_axis(jnp.transpose(send_start, (0, 2, 1)), source, axis=2)
    place_base = jnp.arange(N_POS, dtype=jnp.int32)[:, None, None] * TOK_DEV
    flat_rows = (source * SEQUENCE_SLOTS + place_base + outgoing_offsets + positions[None, None, :] - recv_from).astype(jnp.int32)
    flat_rows = jnp.transpose(flat_rows, (1, 0, 2)).reshape(N_STREAM, SEQUENCE_SLOTS)
    token_flat = tokens_in.reshape(N_STREAM * SEQUENCE_SLOTS, HEADS * HDIM)
    proj_flat = proj_in.reshape(N_STREAM * SEQUENCE_SLOTS, 2 * STATE)
    step_flat = step_raw.reshape(N_STREAM * SEQUENCE_SLOTS, HEADS)
    block_count = SEQUENCE_SLOTS // BLOCK
    block_step = partial(stream_blocks, decay_rates=decay_rates, head_skip_weight=head_skip_weight)

    def one_stream(stream_rows):
        tokens = jnp.take(token_flat, stream_rows, axis=0).reshape(block_count, BLOCK, HEADS * HDIM)
        input_projections = jnp.take(proj_flat, stream_rows, axis=0).reshape(block_count, BLOCK, 2 * STATE)
        steps_raw = jnp.take(step_flat, stream_rows, axis=0).reshape(block_count, BLOCK, HEADS)
        start_state = jnp.zeros((HEADS, STATE, HDIM), jnp.float32)
        scanned = lax.scan(block_step, start_state, (tokens, input_projections, steps_raw))
        return scanned[1].reshape(SEQUENCE_SLOTS, HEADS * HDIM)

    return lax.map(one_stream, flat_rows)
```

```python
import jax
import jax.numpy as jnp
from jax import lax
from jax.experimental import pallas as pl
from jax.experimental.pallas import tpu as pltpu
from jax.sharding import PartitionSpec as P

TILE_HEADS = 8
ROWS = 128
GROUPS = (4, 4, 4, 2, 2)
LOG2E = 1.4426950408889634
VMEM = 40 * 1024 * 1024


def expand(factors, pair, low):
    return jnp.where(low, factors[:, 2 * pair : 2 * pair + 1], factors[:, 2 * pair + 1 : 2 * pair + 2])


def state_kernel(order_ref, arrived_ref, inputs_t_ref, factor_ref, x_ref, carried_ref, scaled_ref):
    x = jnp.dot(order_ref[...], arrived_ref[...], preferred_element_type=jnp.float32)
    x_ref[...] = x.astype(jnp.bfloat16)
    factors = factor_ref[0]
    rows = x.shape[0]
    low = lax.broadcasted_iota(jnp.int32, (rows, 128), 1) < 64
    for pair in range(TILE_HEADS // 2):
        part = slice(128 * pair, 128 * pair + 128)
        scaled_ref[:, part] = (expand(factors, pair, low) * x[:, part]).astype(jnp.bfloat16)
    carried_ref[...] = jnp.dot(
        inputs_t_ref[...], scaled_ref[...], preferred_element_type=jnp.float32
    ).astype(jnp.bfloat16)


def output_kernel(
    x_ref,
    scores_ref,
    readout_ref,
    cum_ref,
    grow_ref,
    source_ref,
    carried_ref,
    coef_ref,
    skip_ref,
    *rest,
):
    out_ref, inherited_ref = rest[-2:]
    peers = carried_ref.shape[0]
    state = coef_ref[0:1, :] * carried_ref[0].astype(jnp.float32)
    for k in range(1, peers):
        state = state + coef_ref[k : k + 1, :] * carried_ref[k].astype(jnp.float32)
    inherited_ref[...] = jnp.dot(
        readout_ref[...], state.astype(jnp.bfloat16), preferred_element_type=jnp.float32
    )
    length = x_ref.shape[0]
    low = lax.broadcasted_iota(jnp.int32, (length, 128), 1) < 64
    low_rows = low[:ROWS]
    causal = lax.broadcasted_iota(jnp.int32, (ROWS, ROWS), 0) >= lax.broadcasted_iota(
        jnp.int32, (ROWS, ROWS), 1
    )
    cum = cum_ref[0]
    grow = grow_ref[0]
    source = source_ref[0]
    for pair in range(TILE_HEADS // 2):
        part = slice(128 * pair, 128 * pair + 128)
        x = x_ref[:, part]
        zero = jnp.zeros_like(x)
        halves = (jnp.where(low, x, zero), jnp.where(low, zero, x))
        for tile in range(length // ROWS):
            here = slice(ROWS * tile, ROWS * tile + ROWS)
            total = expand(grow[here], pair, low_rows) * inherited_ref[here, part]
            total = total + skip_ref[:, part] * x[here].astype(jnp.float32)
            for which in range(2):
                head = 2 * pair + which
                last = cum[here, head : head + 1]
                pieces = []
                if tile:
                    gap = last - source[head : head + 1, : ROWS * tile]
                    pieces.append(
                        (scores_ref[here, : ROWS * tile] * jnp.exp2(gap)).astype(jnp.bfloat16)
                    )
                gap = jnp.where(causal, last - source[head : head + 1, here], -jnp.inf)
                pieces.append((scores_ref[here, here] * jnp.exp2(gap)).astype(jnp.bfloat16))
                weights = pieces[0] if len(pieces) == 1 else jnp.concatenate(pieces, axis=1)
                total = total + jnp.dot(
                    weights,
                    halves[which][: ROWS * (tile + 1)],
                    preferred_element_type=jnp.float32,
                )
            out_ref[here, part] = total.astype(jnp.bfloat16)


def states(order, arrived, inputs_t, factors, first, tiles, tile_cols):
    rows, slots = order.shape
    state_size = inputs_t.shape[0]
    cols = tiles * tile_cols
    return pl.pallas_call(
        state_kernel,
        grid=(tiles,),
        in_specs=[
            pl.BlockSpec((rows, slots), lambda i: (0, 0)),
            pl.BlockSpec((slots, tile_cols), lambda i: (0, i)),
            pl.BlockSpec((state_size, rows), lambda i: (0, 0)),
            pl.BlockSpec((1, rows, TILE_HEADS), lambda i: (first + i, 0, 0)),
        ],
        out_specs=[
            pl.BlockSpec((rows, tile_cols), lambda i: (0, i)),
            pl.BlockSpec((state_size, tile_cols), lambda i: (0, i)),
        ],
        out_shape=[
            jax.ShapeDtypeStruct((rows, cols), jnp.bfloat16),
            jax.ShapeDtypeStruct((state_size, cols), jnp.bfloat16),
        ],
        scratch_shapes=[pltpu.VMEM((rows, tile_cols), jnp.bfloat16)],
        compiler_params=pltpu.CompilerParams(vmem_limit_bytes=VMEM),
        cost_estimate=pl.CostEstimate(
            flops=2 * rows * slots * cols + 2 * rows * state_size * cols,
            bytes_accessed=2 * (slots + rows + state_size) * cols,
            transcendentals=0,
        ),
    )(order, arrived, inputs_t, factors)


def outputs(previous, x, scores, readout, cum, grow, source, carried, coef, skip, first, tiles, tile_cols):
    rows = x.shape[0]
    state_size = readout.shape[1]
    peers = carried.shape[0]
    cols = tiles * tile_cols
    whole = coef.shape[1]
    in_specs = [
        pl.BlockSpec((rows, tile_cols), lambda i: (0, i)),
        pl.BlockSpec((rows, rows), lambda i: (0, 0)),
        pl.BlockSpec((rows, state_size), lambda i: (0, 0)),
        pl.BlockSpec((1, rows, TILE_HEADS), lambda i: (first + i, 0, 0)),
        pl.BlockSpec((1, rows, TILE_HEADS), lambda i: (first + i, 0, 0)),
        pl.BlockSpec((1, TILE_HEADS, rows), lambda i: (first + i, 0, 0)),
        pl.BlockSpec((peers, state_size, tile_cols), lambda i: (0, 0, i)),
        pl.BlockSpec((peers, tile_cols), lambda i: (0, first + i)),
        pl.BlockSpec((1, tile_cols), lambda i: (0, first + i)),
    ]
    operands = [x, scores, readout, cum, grow, source, carried, coef, skip]
    aliases = {}
    if previous is not None:
        in_specs.append(pl.BlockSpec(memory_space=pl.ANY))
        aliases = {len(operands): 0}
        operands.append(previous)
    return pl.pallas_call(
        output_kernel,
        grid=(tiles,),
        in_specs=in_specs,
        out_specs=pl.BlockSpec((rows, tile_cols), lambda i: (0, first + i)),
        out_shape=jax.ShapeDtypeStruct((rows, whole), jnp.bfloat16),
        scratch_shapes=[pltpu.VMEM((rows, tile_cols), jnp.float32)],
        input_output_aliases=aliases,
        compiler_params=pltpu.CompilerParams(vmem_limit_bytes=VMEM),
        cost_estimate=pl.CostEstimate(
            flops=2 * rows * (rows * 3 + state_size) * cols,
            bytes_accessed=2 * (2 * rows + peers * state_size) * cols,
            transcendentals=rows * rows * TILE_HEADS * tiles,
        ),
    )(*operands)


def on_device(tokens_in, proj_in, step_raw, decay_log, head_skip_weight, row_counts):
    streams = lax.axis_size("stream")
    stream = lax.axis_index("stream")
    place = lax.axis_index("pos")
    peers = lax.axis_size("pos")
    tokens = tokens_in[0]
    rows, inner = tokens.shape
    heads = step_raw.shape[2]
    head_size = inner // heads
    state_size = proj_in.shape[2] // 2
    capacity = 3 * rows // (2 * streams)
    slots = streams * capacity
    tile_cols = TILE_HEADS * head_size
    all_tiles = heads // TILE_HEADS

    counts = lax.dynamic_index_in_dim(row_counts, place, 0, keepdims=False)
    sent = lax.dynamic_index_in_dim(counts, stream, 0, keepdims=False)
    received = lax.dynamic_index_in_dim(counts, stream, 1, keepdims=False)
    send_start = jnp.cumsum(sent) - sent
    recv_start = jnp.cumsum(received) - received
    slot = jnp.arange(capacity, dtype=jnp.int32)
    picked = (send_start[:, None] + slot[None, :]).reshape(slots)
    position = jnp.arange(rows, dtype=jnp.int32)
    pack = (picked[:, None] == position[None, :]).astype(jnp.bfloat16)
    landed = jnp.where(
        slot[None, :] < received[:, None], recv_start[:, None] + slot[None, :], -1
    ).reshape(slots)
    order = (position[:, None] == landed[None, :]).astype(jnp.bfloat16)

    def exchange(block):
        packed = jnp.dot(pack, block, preferred_element_type=jnp.bfloat16)
        packed = packed.reshape(streams, capacity, block.shape[1])
        arrived = lax.all_to_all(packed, "stream", split_axis=0, concat_axis=0, tiled=True)
        return arrived.reshape(slots, block.shape[1])

    small = exchange(jnp.concatenate([proj_in[0], step_raw[0]], axis=1))
    bounds = []
    first = 0
    for share in GROUPS:
        tiles = share * all_tiles // 16
        bounds.append((first, tiles))
        first += tiles
    arrivals = [
        exchange(tokens[:, a * tile_cols : (a + n) * tile_cols]) for a, n in bounds
    ]

    small = jnp.dot(order, small, preferred_element_type=jnp.bfloat16)
    inputs = small[:, :state_size]
    readout = small[:, state_size : 2 * state_size]
    steps = jax.nn.softplus(small[:, 2 * state_size :].astype(jnp.float32))
    cumulated = jnp.cumsum(steps * -jnp.exp(decay_log)[None, :], axis=0)
    ending = cumulated[-1]
    scores = jnp.dot(readout, inputs.T, preferred_element_type=jnp.float32)
    inputs_t = inputs.T

    def by_tile(array):
        return jnp.moveaxis(array.reshape(rows, all_tiles, TILE_HEADS), 1, 0)

    factors = by_tile(jnp.exp(ending[None, :] - cumulated) * steps)
    grow = by_tile(jnp.exp(cumulated))
    cum = by_tile(cumulated * LOG2E)
    source = (cumulated * LOG2E - jnp.log2(steps)).T.reshape(all_tiles, TILE_HEADS, rows)

    endings = lax.all_gather(ending, "pos")
    places = jnp.arange(peers, dtype=jnp.int32)
    between = (places[None, :] > places[:, None]) & (places[None, :] < place)
    exponent = jnp.sum(jnp.where(between[:, :, None], endings[None], 0.0), axis=1)
    coef = jnp.where((places < place)[:, None], jnp.exp(exponent), 0.0)
    coef = jnp.repeat(coef, head_size, axis=1)
    skip = jnp.repeat(head_skip_weight, head_size)[None, :]

    result = None
    for (a, n), arrived in zip(bounds, arrivals):
        x, carried = states(order, arrived, inputs_t, factors, a, n, tile_cols)
        gathered = lax.all_gather(carried, "pos")
        result = outputs(
            result, x, scores, readout, cum, grow, source, gathered, coef, skip, a, n, tile_cols
        )
    return result[None]


def solution(mesh):
    in_specs = (
        P("stream", "pos", None),
        P("stream", "pos", None),
        P("stream", "pos", None),
        P(),
        P(),
        P(),
    )
    return jax.shard_map(
        on_device,
        mesh=mesh,
        in_specs=in_specs,
        out_specs=P("stream", "pos", None),
        check_vma=False,
    )
```

```python
import jax
import jax.numpy as jnp
from jax import lax
from jax.experimental import pallas as pl
from jax.experimental.pallas import tpu as pltpu
from jax.sharding import PartitionSpec as P

TILE_HEADS = 8
ROWS = 128
GROUPS = (4, 9, 3)
LOG2E = 1.4426950408889634
VMEM = 40 * 1024 * 1024


def expand(factors, pair, low):
    return jnp.where(low, factors[:, 2 * pair : 2 * pair + 1], factors[:, 2 * pair + 1 : 2 * pair + 2])


def state_kernel(order_ref, arrived_ref, inputs_t_ref, factor_ref, x_ref, carried_ref, scaled_ref):
    x = jnp.dot(order_ref[...], arrived_ref[...], preferred_element_type=jnp.float32)
    x_ref[...] = x.astype(jnp.bfloat16)
    factors = factor_ref[0]
    rows = x.shape[0]
    low = lax.broadcasted_iota(jnp.int32, (rows, 128), 1) < 64
    for pair in range(TILE_HEADS // 2):
        part = slice(128 * pair, 128 * pair + 128)
        scaled_ref[:, part] = (expand(factors, pair, low) * x[:, part]).astype(jnp.bfloat16)
    carried_ref[...] = jnp.dot(
        inputs_t_ref[...], scaled_ref[...], preferred_element_type=jnp.float32
    ).astype(jnp.bfloat16)


def output_kernel(
    x_ref,
    scores_ref,
    readout_ref,
    cum_ref,
    grow_ref,
    source_ref,
    carried_ref,
    coef_ref,
    skip_ref,
    *rest,
):
    out_ref, inherited_ref = rest[-2:]
    peers = carried_ref.shape[0]
    state = coef_ref[0:1, :] * carried_ref[0].astype(jnp.float32)
    for k in range(1, peers):
        state = state + coef_ref[k : k + 1, :] * carried_ref[k].astype(jnp.float32)
    inherited_ref[...] = jnp.dot(
        readout_ref[...], state.astype(jnp.bfloat16), preferred_element_type=jnp.float32
    )
    length = x_ref.shape[0]
    low = lax.broadcasted_iota(jnp.int32, (length, 128), 1) < 64
    low_rows = low[:ROWS]
    causal = lax.broadcasted_iota(jnp.int32, (ROWS, ROWS), 0) >= lax.broadcasted_iota(
        jnp.int32, (ROWS, ROWS), 1
    )
    cum = cum_ref[0]
    grow = grow_ref[0]
    source = source_ref[0]
    for pair in range(TILE_HEADS // 2):
        part = slice(128 * pair, 128 * pair + 128)
        x = x_ref[:, part]
        zero = jnp.zeros_like(x)
        halves = (jnp.where(low, x, zero), jnp.where(low, zero, x))
        for tile in range(length // ROWS):
            here = slice(ROWS * tile, ROWS * tile + ROWS)
            total = expand(grow[here], pair, low_rows) * inherited_ref[here, part]
            total = total + skip_ref[:, part] * x[here].astype(jnp.float32)
            for which in range(2):
                head = 2 * pair + which
                last = cum[here, head : head + 1]
                pieces = []
                if tile:
                    gap = last - source[head : head + 1, : ROWS * tile]
                    pieces.append(
                        (scores_ref[here, : ROWS * tile] * jnp.exp2(gap)).astype(jnp.bfloat16)
                    )
                gap = jnp.where(causal, last - source[head : head + 1, here], -jnp.inf)
                pieces.append((scores_ref[here, here] * jnp.exp2(gap)).astype(jnp.bfloat16))
                weights = pieces[0] if len(pieces) == 1 else jnp.concatenate(pieces, axis=1)
                total = total + jnp.dot(
                    weights,
                    halves[which][: ROWS * (tile + 1)],
                    preferred_element_type=jnp.float32,
                )
            out_ref[here, part] = total.astype(jnp.bfloat16)


def states(order, arrived, inputs_t, factors, first, tiles, tile_cols):
    rows, slots = order.shape
    state_size = inputs_t.shape[0]
    cols = tiles * tile_cols
    return pl.pallas_call(
        state_kernel,
        grid=(tiles,),
        in_specs=[
            pl.BlockSpec((rows, slots), lambda i: (0, 0)),
            pl.BlockSpec((slots, tile_cols), lambda i: (0, i)),
            pl.BlockSpec((state_size, rows), lambda i: (0, 0)),
            pl.BlockSpec((1, rows, TILE_HEADS), lambda i: (first + i, 0, 0)),
        ],
        out_specs=[
            pl.BlockSpec((rows, tile_cols), lambda i: (0, i)),
            pl.BlockSpec((state_size, tile_cols), lambda i: (0, i)),
        ],
        out_shape=[
            jax.ShapeDtypeStruct((rows, cols), jnp.bfloat16),
            jax.ShapeDtypeStruct((state_size, cols), jnp.bfloat16),
        ],
        scratch_shapes=[pltpu.VMEM((rows, tile_cols), jnp.bfloat16)],
        compiler_params=pltpu.CompilerParams(vmem_limit_bytes=VMEM),
        cost_estimate=pl.CostEstimate(
            flops=2 * rows * slots * cols + 2 * rows * state_size * cols,
            bytes_accessed=2 * (slots + rows + state_size) * cols,
            transcendentals=0,
        ),
    )(order, arrived, inputs_t, factors)


def outputs(previous, x, scores, readout, cum, grow, source, carried, coef, skip, first, tiles, tile_cols):
    rows = x.shape[0]
    state_size = readout.shape[1]
    peers = carried.shape[0]
    cols = tiles * tile_cols
    whole = coef.shape[1]
    in_specs = [
        pl.BlockSpec((rows, tile_cols), lambda i: (0, i)),
        pl.BlockSpec((rows, rows), lambda i: (0, 0)),
        pl.BlockSpec((rows, state_size), lambda i: (0, 0)),
        pl.BlockSpec((1, rows, TILE_HEADS), lambda i: (first + i, 0, 0)),
        pl.BlockSpec((1, rows, TILE_HEADS), lambda i: (first + i, 0, 0)),
        pl.BlockSpec((1, TILE_HEADS, rows), lambda i: (first + i, 0, 0)),
        pl.BlockSpec((peers, state_size, tile_cols), lambda i: (0, 0, i)),
        pl.BlockSpec((peers, tile_cols), lambda i: (0, first + i)),
        pl.BlockSpec((1, tile_cols), lambda i: (0, first + i)),
    ]
    operands = [x, scores, readout, cum, grow, source, carried, coef, skip]
    aliases = {}
    if previous is not None:
        in_specs.append(pl.BlockSpec(memory_space=pl.ANY))
        aliases = {len(operands): 0}
        operands.append(previous)
    return pl.pallas_call(
        output_kernel,
        grid=(tiles,),
        in_specs=in_specs,
        out_specs=pl.BlockSpec((rows, tile_cols), lambda i: (0, first + i)),
        out_shape=jax.ShapeDtypeStruct((rows, whole), jnp.bfloat16),
        scratch_shapes=[pltpu.VMEM((rows, tile_cols), jnp.float32)],
        input_output_aliases=aliases,
        compiler_params=pltpu.CompilerParams(vmem_limit_bytes=VMEM),
        cost_estimate=pl.CostEstimate(
            flops=2 * rows * (rows * 3 + state_size) * cols,
            bytes_accessed=2 * (2 * rows + peers * state_size) * cols,
            transcendentals=rows * rows * TILE_HEADS * tiles,
        ),
    )(*operands)


def on_device(tokens_in, proj_in, step_raw, decay_log, head_skip_weight, row_counts):
    streams = lax.axis_size("stream")
    stream = lax.axis_index("stream")
    place = lax.axis_index("pos")
    peers = lax.axis_size("pos")
    tokens = tokens_in[0]
    rows, inner = tokens.shape
    heads = step_raw.shape[2]
    head_size = inner // heads
    state_size = proj_in.shape[2] // 2
    capacity = 3 * rows // (2 * streams)
    slots = streams * capacity
    tile_cols = TILE_HEADS * head_size
    all_tiles = heads // TILE_HEADS

    counts = lax.dynamic_index_in_dim(row_counts, place, 0, keepdims=False)
    sent = lax.dynamic_index_in_dim(counts, stream, 0, keepdims=False)
    received = lax.dynamic_index_in_dim(counts, stream, 1, keepdims=False)
    send_start = jnp.cumsum(sent) - sent
    recv_start = jnp.cumsum(received) - received
    slot = jnp.arange(capacity, dtype=jnp.int32)
    picked = (send_start[:, None] + slot[None, :]).reshape(slots)
    position = jnp.arange(rows, dtype=jnp.int32)
    pack = (picked[:, None] == position[None, :]).astype(jnp.bfloat16)
    landed = jnp.where(
        slot[None, :] < received[:, None], recv_start[:, None] + slot[None, :], -1
    ).reshape(slots)
    order = (position[:, None] == landed[None, :]).astype(jnp.bfloat16)

    def exchange(block):
        packed = jnp.dot(pack, block, preferred_element_type=jnp.bfloat16)
        packed = packed.reshape(streams, capacity, block.shape[1])
        arrived = lax.all_to_all(packed, "stream", split_axis=0, concat_axis=0, tiled=True)
        return arrived.reshape(slots, block.shape[1])

    bounds = []
    first = 0
    for share in GROUPS:
        tiles = share * all_tiles // 16
        bounds.append((first, tiles))
        first += tiles

    def columns(group):
        a, n = bounds[group]
        return tokens[:, a * tile_cols : (a + n) * tile_cols]

    arrivals = [
        exchange(jnp.concatenate([columns(0), proj_in[0], step_raw[0]], axis=1)),
    ] + [exchange(columns(group)) for group in range(1, len(bounds))]
    ahead = bounds[0][1] * tile_cols
    small = jnp.dot(order, arrivals[0][:, ahead:], preferred_element_type=jnp.bfloat16)
    inputs = small[:, :state_size]
    readout = small[:, state_size : 2 * state_size]
    steps = jax.nn.softplus(small[:, 2 * state_size :].astype(jnp.float32))
    cumulated = jnp.cumsum(steps * -jnp.exp(decay_log)[None, :], axis=0)
    ending = cumulated[-1]
    scores = jnp.dot(readout, inputs.T, preferred_element_type=jnp.float32)
    inputs_t = inputs.T

    def by_tile(array):
        return jnp.moveaxis(array.reshape(rows, all_tiles, TILE_HEADS), 1, 0)

    factors = by_tile(jnp.exp(ending[None, :] - cumulated) * steps)
    grow = by_tile(jnp.exp(cumulated))
    cum = by_tile(cumulated * LOG2E)
    source = (cumulated * LOG2E - jnp.log2(steps)).T.reshape(all_tiles, TILE_HEADS, rows)

    endings = lax.all_gather(ending, "pos")
    places = jnp.arange(peers, dtype=jnp.int32)
    between = (places[None, :] > places[:, None]) & (places[None, :] < place)
    exponent = jnp.sum(jnp.where(between[:, :, None], endings[None], 0.0), axis=1)
    coef = jnp.where((places < place)[:, None], jnp.exp(exponent), 0.0)
    coef = jnp.repeat(coef, head_size, axis=1)
    skip = jnp.repeat(head_skip_weight, head_size)[None, :]

    result = None
    for group, (a, n) in enumerate(bounds):
        arrived = arrivals[group]
        if result is not None:
            arrived, result = lax.optimization_barrier((arrived, result))
        x, carried = states(order, arrived, inputs_t, factors, a, n, tile_cols)
        gathered = lax.all_gather(carried, "pos")
        result = outputs(
            result, x, scores, readout, cum, grow, source, gathered, coef, skip, a, n, tile_cols
        )
    return result[None]


def solution(mesh):
    in_specs = (
        P("stream", "pos", None),
        P("stream", "pos", None),
        P("stream", "pos", None),
        P(),
        P(),
        P(),
    )
    return jax.shard_map(
        on_device,
        mesh=mesh,
        in_specs=in_specs,
        out_specs=P("stream", "pos", None),
        check_vma=False,
    )
```

```python
import jax
import jax.numpy as jnp
from jax import lax
from jax.experimental import pallas as pl
from jax.experimental.pallas import tpu as pltpu
from jax.sharding import PartitionSpec as P

TILE_HEADS = 8
ROWS = 128
GROUPS = (5, 8, 3)
LOG2E = 1.4426950408889634
VMEM = 58 * 1024 * 1024


def expand(factors, pair, low):
    return jnp.where(low, factors[:, 2 * pair : 2 * pair + 1], factors[:, 2 * pair + 1 : 2 * pair + 2])


def state_kernel(order_ref, arrived_ref, inputs_t_ref, factor_ref, x_ref, carried_ref, scaled_ref):
    x = jnp.dot(order_ref[...], arrived_ref[...], preferred_element_type=jnp.float32)
    x_ref[...] = x.astype(jnp.bfloat16)
    factors = factor_ref[0]
    rows = x.shape[0]
    low = lax.broadcasted_iota(jnp.int32, (rows, 128), 1) < 64
    for pair in range(TILE_HEADS // 2):
        part = slice(128 * pair, 128 * pair + 128)
        scaled_ref[:, part] = (expand(factors, pair, low) * x[:, part]).astype(jnp.bfloat16)
    carried_ref[...] = jnp.dot(
        inputs_t_ref[...], scaled_ref[...], preferred_element_type=jnp.float32
    ).astype(jnp.bfloat16)


def output_kernel(
    x_ref,
    scores_ref,
    readout_ref,
    cum_ref,
    grow_ref,
    source_ref,
    carried_ref,
    coef_ref,
    skip_ref,
    *rest,
):
    out_ref, inherited_ref = rest[-2:]
    peers = carried_ref.shape[0]
    state = coef_ref[0:1, :] * carried_ref[0].astype(jnp.float32)
    for k in range(1, peers):
        state = state + coef_ref[k : k + 1, :] * carried_ref[k].astype(jnp.float32)
    inherited_ref[...] = jnp.dot(
        readout_ref[...], state.astype(jnp.bfloat16), preferred_element_type=jnp.float32
    )
    length = x_ref.shape[0]
    low = lax.broadcasted_iota(jnp.int32, (length, 128), 1) < 64
    low_rows = low[:ROWS]
    causal = lax.broadcasted_iota(jnp.int32, (ROWS, ROWS), 0) >= lax.broadcasted_iota(
        jnp.int32, (ROWS, ROWS), 1
    )
    cum = cum_ref[0]
    grow = grow_ref[0]
    source = source_ref[0]
    for pair in range(TILE_HEADS // 2):
        part = slice(128 * pair, 128 * pair + 128)
        x = x_ref[:, part]
        zero = jnp.zeros_like(x)
        halves = (jnp.where(low, x, zero), jnp.where(low, zero, x))
        for tile in range(length // ROWS):
            here = slice(ROWS * tile, ROWS * tile + ROWS)
            total = expand(grow[here], pair, low_rows) * inherited_ref[here, part]
            total = total + skip_ref[:, part] * x[here].astype(jnp.float32)
            for which in range(2):
                head = 2 * pair + which
                last = cum[here, head : head + 1]
                pieces = []
                if tile:
                    gap = last - source[head : head + 1, : ROWS * tile]
                    pieces.append(
                        (scores_ref[here, : ROWS * tile] * jnp.exp2(gap)).astype(jnp.bfloat16)
                    )
                gap = jnp.where(causal, last - source[head : head + 1, here], -jnp.inf)
                pieces.append((scores_ref[here, here] * jnp.exp2(gap)).astype(jnp.bfloat16))
                weights = pieces[0] if len(pieces) == 1 else jnp.concatenate(pieces, axis=1)
                total = total + jnp.dot(
                    weights,
                    halves[which][: ROWS * (tile + 1)],
                    preferred_element_type=jnp.float32,
                )
            out_ref[here, part] = total.astype(jnp.bfloat16)


def states(order, arrived, inputs_t, factors, first, tiles, tile_cols):
    rows, slots = order.shape
    state_size = inputs_t.shape[0]
    cols = tiles * tile_cols
    return pl.pallas_call(
        state_kernel,
        grid=(tiles,),
        in_specs=[
            pl.BlockSpec((rows, slots), lambda i: (0, 0)),
            pl.BlockSpec((slots, tile_cols), lambda i: (0, i)),
            pl.BlockSpec((state_size, rows), lambda i: (0, 0)),
            pl.BlockSpec((1, rows, TILE_HEADS), lambda i: (first + i, 0, 0)),
        ],
        out_specs=[
            pl.BlockSpec((rows, tile_cols), lambda i: (0, i)),
            pl.BlockSpec((state_size, tile_cols), lambda i: (0, i)),
        ],
        out_shape=[
            jax.ShapeDtypeStruct((rows, cols), jnp.bfloat16),
            jax.ShapeDtypeStruct((state_size, cols), jnp.bfloat16),
        ],
        scratch_shapes=[pltpu.VMEM((rows, tile_cols), jnp.bfloat16)],
        compiler_params=pltpu.CompilerParams(vmem_limit_bytes=VMEM),
        cost_estimate=pl.CostEstimate(
            flops=2 * rows * slots * cols + 2 * rows * state_size * cols,
            bytes_accessed=2 * (slots + rows + state_size) * cols,
            transcendentals=0,
        ),
    )(order, arrived, inputs_t, factors)


def outputs(previous, x, scores, readout, cum, grow, source, carried, coef, skip, first, tiles, tile_cols):
    rows = x.shape[0]
    state_size = readout.shape[1]
    peers = carried.shape[0]
    cols = tiles * tile_cols
    whole = coef.shape[1]
    in_specs = [
        pl.BlockSpec((rows, tile_cols), lambda i: (0, i)),
        pl.BlockSpec((rows, rows), lambda i: (0, 0)),
        pl.BlockSpec((rows, state_size), lambda i: (0, 0)),
        pl.BlockSpec((1, rows, TILE_HEADS), lambda i: (first + i, 0, 0)),
        pl.BlockSpec((1, rows, TILE_HEADS), lambda i: (first + i, 0, 0)),
        pl.BlockSpec((1, TILE_HEADS, rows), lambda i: (first + i, 0, 0)),
        pl.BlockSpec((peers, state_size, tile_cols), lambda i: (0, 0, i)),
        pl.BlockSpec((peers, tile_cols), lambda i: (0, first + i)),
        pl.BlockSpec((1, tile_cols), lambda i: (0, first + i)),
    ]
    operands = [x, scores, readout, cum, grow, source, carried, coef, skip]
    aliases = {}
    if previous is not None:
        in_specs.append(pl.BlockSpec(memory_space=pl.ANY))
        aliases = {len(operands): 0}
        operands.append(previous)
    return pl.pallas_call(
        output_kernel,
        grid=(tiles,),
        in_specs=in_specs,
        out_specs=pl.BlockSpec((rows, tile_cols), lambda i: (0, first + i)),
        out_shape=jax.ShapeDtypeStruct((rows, whole), jnp.bfloat16),
        scratch_shapes=[pltpu.VMEM((rows, tile_cols), jnp.float32)],
        input_output_aliases=aliases,
        compiler_params=pltpu.CompilerParams(vmem_limit_bytes=VMEM),
        cost_estimate=pl.CostEstimate(
            flops=2 * rows * (rows * 3 + state_size) * cols,
            bytes_accessed=2 * (2 * rows + peers * state_size) * cols,
            transcendentals=rows * rows * TILE_HEADS * tiles,
        ),
    )(*operands)


def on_device(tokens_in, proj_in, step_raw, decay_log, head_skip_weight, row_counts):
    streams = lax.axis_size("stream")
    stream = lax.axis_index("stream")
    place = lax.axis_index("pos")
    peers = lax.axis_size("pos")
    tokens = tokens_in[0]
    rows, inner = tokens.shape
    heads = step_raw.shape[2]
    head_size = inner // heads
    state_size = proj_in.shape[2] // 2
    capacity = 3 * rows // (2 * streams)
    slots = streams * capacity
    tile_cols = TILE_HEADS * head_size
    all_tiles = heads // TILE_HEADS

    counts = lax.dynamic_index_in_dim(row_counts, place, 0, keepdims=False)
    sent = lax.dynamic_index_in_dim(counts, stream, 0, keepdims=False)
    received = lax.dynamic_index_in_dim(counts, stream, 1, keepdims=False)
    send_start = jnp.cumsum(sent) - sent
    recv_start = jnp.cumsum(received) - received
    slot = jnp.arange(capacity, dtype=jnp.int32)
    picked = (send_start[:, None] + slot[None, :]).reshape(slots)
    position = jnp.arange(rows, dtype=jnp.int32)
    pack = (picked[:, None] == position[None, :]).astype(jnp.bfloat16)
    landed = jnp.where(
        slot[None, :] < received[:, None], recv_start[:, None] + slot[None, :], -1
    ).reshape(slots)
    order = (position[:, None] == landed[None, :]).astype(jnp.bfloat16)

    def exchange(block):
        packed = jnp.dot(pack, block, preferred_element_type=jnp.bfloat16)
        packed = packed.reshape(streams, capacity, block.shape[1])
        arrived = lax.all_to_all(packed, "stream", split_axis=0, concat_axis=0, tiled=True)
        return arrived.reshape(slots, block.shape[1])

    bounds = []
    first = 0
    for share in GROUPS:
        tiles = share * all_tiles // 16
        bounds.append((first, tiles))
        first += tiles

    def columns(group):
        a, n = bounds[group]
        return tokens[:, a * tile_cols : (a + n) * tile_cols]

    arrivals = [
        exchange(jnp.concatenate([columns(0), proj_in[0], step_raw[0]], axis=1)),
    ] + [exchange(columns(group)) for group in range(1, len(bounds))]
    ahead = bounds[0][1] * tile_cols
    small = jnp.dot(order, arrivals[0][:, ahead:], preferred_element_type=jnp.bfloat16)
    inputs = small[:, :state_size]
    readout = small[:, state_size : 2 * state_size]
    steps = jax.nn.softplus(small[:, 2 * state_size :].astype(jnp.float32))
    cumulated = jnp.cumsum(steps * -jnp.exp(decay_log)[None, :], axis=0)
    ending = cumulated[-1]
    scores = jnp.dot(readout, inputs.T, preferred_element_type=jnp.float32)
    inputs_t = inputs.T

    def by_tile(array):
        return jnp.moveaxis(array.reshape(rows, all_tiles, TILE_HEADS), 1, 0)

    factors = by_tile(jnp.exp(ending[None, :] - cumulated) * steps)
    grow = by_tile(jnp.exp(cumulated))
    cum = by_tile(cumulated * LOG2E)
    source = (cumulated * LOG2E - jnp.log2(steps)).T.reshape(all_tiles, TILE_HEADS, rows)

    endings = lax.all_gather(ending, "pos")
    places = jnp.arange(peers, dtype=jnp.int32)
    between = (places[None, :] > places[:, None]) & (places[None, :] < place)
    exponent = jnp.sum(jnp.where(between[:, :, None], endings[None], 0.0), axis=1)
    coef = jnp.where((places < place)[:, None], jnp.exp(exponent), 0.0)
    coef = jnp.repeat(coef, head_size, axis=1)
    skip = jnp.repeat(head_skip_weight, head_size)[None, :]

    result = None
    for group, (a, n) in enumerate(bounds):
        arrived = arrivals[group]
        if result is not None and group + 1 < len(bounds):
            arrived, result = lax.optimization_barrier((arrived, result))
        x, carried = states(order, arrived, inputs_t, factors, a, n, tile_cols)
        gathered = lax.all_gather(carried, "pos")
        result = outputs(
            result, x, scores, readout, cum, grow, source, gathered, coef, skip, a, n, tile_cols
        )
    return result[None]


def solution(mesh):
    in_specs = (
        P("stream", "pos", None),
        P("stream", "pos", None),
        P("stream", "pos", None),
        P(),
        P(),
        P(),
    )
    return jax.shard_map(
        on_device,
        mesh=mesh,
        in_specs=in_specs,
        out_specs=P("stream", "pos", None),
        check_vma=False,
    )
```

```python
import jax
import jax.numpy as jnp
from jax import lax
from jax.experimental import pallas as pl
from jax.experimental.pallas import tpu as pltpu
from jax.sharding import PartitionSpec as P

TILE_HEADS = 8
ROWS = 128
GROUPS = (7, 8, 1)
LOG2E = 1.4426950408889634
VMEM = 58 * 1024 * 1024


def expand(factors, pair, low):
    return jnp.where(low, factors[:, 2 * pair : 2 * pair + 1], factors[:, 2 * pair + 1 : 2 * pair + 2])


def state_kernel(order_ref, arrived_ref, inputs_t_ref, factor_ref, x_ref, carried_ref, scaled_ref):
    x = jnp.dot(order_ref[...], arrived_ref[...], preferred_element_type=jnp.float32)
    x_ref[...] = x.astype(jnp.bfloat16)
    factors = factor_ref[0]
    rows = x.shape[0]
    low = lax.broadcasted_iota(jnp.int32, (rows, 128), 1) < 64
    for pair in range(TILE_HEADS // 2):
        part = slice(128 * pair, 128 * pair + 128)
        scaled_ref[:, part] = (expand(factors, pair, low) * x[:, part]).astype(jnp.bfloat16)
    carried_ref[...] = jnp.dot(
        inputs_t_ref[...], scaled_ref[...], preferred_element_type=jnp.float32
    ).astype(jnp.bfloat16)


def output_kernel(
    x_ref,
    scores_ref,
    readout_ref,
    cum_ref,
    grow_ref,
    source_ref,
    carried_ref,
    coef_ref,
    skip_ref,
    *rest,
):
    out_ref, inherited_ref = rest[-2:]
    peers = carried_ref.shape[0]
    state = coef_ref[0:1, :] * carried_ref[0].astype(jnp.float32)
    for k in range(1, peers):
        state = state + coef_ref[k : k + 1, :] * carried_ref[k].astype(jnp.float32)
    inherited_ref[...] = jnp.dot(
        readout_ref[...], state.astype(jnp.bfloat16), preferred_element_type=jnp.float32
    )
    length = x_ref.shape[0]
    low = lax.broadcasted_iota(jnp.int32, (length, 128), 1) < 64
    low_rows = low[:ROWS]
    causal = lax.broadcasted_iota(jnp.int32, (ROWS, ROWS), 0) >= lax.broadcasted_iota(
        jnp.int32, (ROWS, ROWS), 1
    )
    cum = cum_ref[0]
    grow = grow_ref[0]
    source = source_ref[0]
    for pair in range(TILE_HEADS // 2):
        part = slice(128 * pair, 128 * pair + 128)
        x = x_ref[:, part]
        zero = jnp.zeros_like(x)
        halves = (jnp.where(low, x, zero), jnp.where(low, zero, x))
        for tile in range(length // ROWS):
            here = slice(ROWS * tile, ROWS * tile + ROWS)
            total = expand(grow[here], pair, low_rows) * inherited_ref[here, part]
            total = total + skip_ref[:, part] * x[here].astype(jnp.float32)
            for which in range(2):
                head = 2 * pair + which
                last = cum[here, head : head + 1]
                pieces = []
                if tile:
                    gap = last - source[head : head + 1, : ROWS * tile]
                    pieces.append(
                        (scores_ref[here, : ROWS * tile] * jnp.exp2(gap)).astype(jnp.bfloat16)
                    )
                gap = jnp.where(causal, last - source[head : head + 1, here], -jnp.inf)
                pieces.append((scores_ref[here, here] * jnp.exp2(gap)).astype(jnp.bfloat16))
                weights = pieces[0] if len(pieces) == 1 else jnp.concatenate(pieces, axis=1)
                total = total + jnp.dot(
                    weights,
                    halves[which][: ROWS * (tile + 1)],
                    preferred_element_type=jnp.float32,
                )
            out_ref[here, part] = total.astype(jnp.bfloat16)


def states(order, arrived, inputs_t, factors, first, tiles, tile_cols):
    rows, slots = order.shape
    state_size = inputs_t.shape[0]
    cols = tiles * tile_cols
    return pl.pallas_call(
        state_kernel,
        grid=(tiles,),
        in_specs=[
            pl.BlockSpec((rows, slots), lambda i: (0, 0)),
            pl.BlockSpec((slots, tile_cols), lambda i: (0, i)),
            pl.BlockSpec((state_size, rows), lambda i: (0, 0)),
            pl.BlockSpec((1, rows, TILE_HEADS), lambda i: (first + i, 0, 0)),
        ],
        out_specs=[
            pl.BlockSpec((rows, tile_cols), lambda i: (0, i)),
            pl.BlockSpec((state_size, tile_cols), lambda i: (0, i)),
        ],
        out_shape=[
            jax.ShapeDtypeStruct((rows, cols), jnp.bfloat16),
            jax.ShapeDtypeStruct((state_size, cols), jnp.bfloat16),
        ],
        scratch_shapes=[pltpu.VMEM((rows, tile_cols), jnp.bfloat16)],
        compiler_params=pltpu.CompilerParams(vmem_limit_bytes=VMEM),
        cost_estimate=pl.CostEstimate(
            flops=2 * rows * slots * cols + 2 * rows * state_size * cols,
            bytes_accessed=2 * (slots + rows + state_size) * cols,
            transcendentals=0,
        ),
    )(order, arrived, inputs_t, factors)


def outputs(previous, x, scores, readout, cum, grow, source, carried, coef, skip, first, tiles, tile_cols):
    rows = x.shape[0]
    state_size = readout.shape[1]
    peers = carried.shape[0]
    cols = tiles * tile_cols
    whole = coef.shape[1]
    in_specs = [
        pl.BlockSpec((rows, tile_cols), lambda i: (0, i)),
        pl.BlockSpec((rows, rows), lambda i: (0, 0)),
        pl.BlockSpec((rows, state_size), lambda i: (0, 0)),
        pl.BlockSpec((1, rows, TILE_HEADS), lambda i: (first + i, 0, 0)),
        pl.BlockSpec((1, rows, TILE_HEADS), lambda i: (first + i, 0, 0)),
        pl.BlockSpec((1, TILE_HEADS, rows), lambda i: (first + i, 0, 0)),
        pl.BlockSpec((peers, state_size, tile_cols), lambda i: (0, 0, i)),
        pl.BlockSpec((peers, tile_cols), lambda i: (0, first + i)),
        pl.BlockSpec((1, tile_cols), lambda i: (0, first + i)),
    ]
    operands = [x, scores, readout, cum, grow, source, carried, coef, skip]
    aliases = {}
    if previous is not None:
        in_specs.append(pl.BlockSpec(memory_space=pl.ANY))
        aliases = {len(operands): 0}
        operands.append(previous)
    return pl.pallas_call(
        output_kernel,
        grid=(tiles,),
        in_specs=in_specs,
        out_specs=pl.BlockSpec((rows, tile_cols), lambda i: (0, first + i)),
        out_shape=jax.ShapeDtypeStruct((rows, whole), jnp.bfloat16),
        scratch_shapes=[pltpu.VMEM((rows, tile_cols), jnp.float32)],
        input_output_aliases=aliases,
        compiler_params=pltpu.CompilerParams(vmem_limit_bytes=VMEM),
        cost_estimate=pl.CostEstimate(
            flops=2 * rows * (rows * 3 + state_size) * cols,
            bytes_accessed=2 * (2 * rows + peers * state_size) * cols,
            transcendentals=rows * rows * TILE_HEADS * tiles,
        ),
    )(*operands)


def on_device(tokens_in, proj_in, step_raw, decay_log, head_skip_weight, row_counts):
    streams = lax.axis_size("stream")
    stream = lax.axis_index("stream")
    place = lax.axis_index("pos")
    peers = lax.axis_size("pos")
    tokens = tokens_in[0]
    rows, inner = tokens.shape
    heads = step_raw.shape[2]
    head_size = inner // heads
    state_size = proj_in.shape[2] // 2
    capacity = 3 * rows // (2 * streams)
    slots = streams * capacity
    tile_cols = TILE_HEADS * head_size
    all_tiles = heads // TILE_HEADS

    counts = lax.dynamic_index_in_dim(row_counts, place, 0, keepdims=False)
    sent = lax.dynamic_index_in_dim(counts, stream, 0, keepdims=False)
    received = lax.dynamic_index_in_dim(counts, stream, 1, keepdims=False)
    send_start = jnp.cumsum(sent) - sent
    recv_start = jnp.cumsum(received) - received
    slot = jnp.arange(capacity, dtype=jnp.int32)
    picked = (send_start[:, None] + slot[None, :]).reshape(slots)
    position = jnp.arange(rows, dtype=jnp.int32)
    pack = (picked[:, None] == position[None, :]).astype(jnp.bfloat16)
    landed = jnp.where(
        slot[None, :] < received[:, None], recv_start[:, None] + slot[None, :], -1
    ).reshape(slots)
    order = (position[:, None] == landed[None, :]).astype(jnp.bfloat16)

    def packed(block):
        return jnp.dot(pack, block, preferred_element_type=jnp.bfloat16)

    def exchange(block):
        width = block.shape[1]
        block = block.reshape(streams, capacity, width)
        arrived = lax.all_to_all(block, "stream", split_axis=0, concat_axis=0, tiled=True)
        return arrived.reshape(slots, width)

    bounds = []
    first = 0
    for share in GROUPS:
        tiles = share * all_tiles // 16
        bounds.append((first, tiles))
        first += tiles

    def columns(group):
        a, n = bounds[group]
        return tokens[:, a * tile_cols : (a + n) * tile_cols]

    leading = packed(jnp.concatenate([columns(0), proj_in[0], step_raw[0]], axis=1))
    later = lax.optimization_barrier([packed(columns(g)) for g in range(1, len(bounds))])
    arrivals = [exchange(block) for block in [leading, *later]]
    ahead = bounds[0][1] * tile_cols
    small = jnp.dot(order, arrivals[0][:, ahead:], preferred_element_type=jnp.bfloat16)
    inputs = small[:, :state_size]
    readout = small[:, state_size : 2 * state_size]
    steps = jax.nn.softplus(small[:, 2 * state_size :].astype(jnp.float32))
    cumulated = jnp.cumsum(steps * -jnp.exp(decay_log)[None, :], axis=0)
    ending = cumulated[-1]
    scores = jnp.dot(readout, inputs.T, preferred_element_type=jnp.float32)
    inputs_t = inputs.T

    def by_tile(array):
        return jnp.moveaxis(array.reshape(rows, all_tiles, TILE_HEADS), 1, 0)

    factors = by_tile(jnp.exp(ending[None, :] - cumulated) * steps)
    grow = by_tile(jnp.exp(cumulated))
    cum = by_tile(cumulated * LOG2E)
    source = (cumulated * LOG2E - jnp.log2(steps)).T.reshape(all_tiles, TILE_HEADS, rows)

    endings = lax.all_gather(ending, "pos")
    places = jnp.arange(peers, dtype=jnp.int32)
    between = (places[None, :] > places[:, None]) & (places[None, :] < place)
    exponent = jnp.sum(jnp.where(between[:, :, None], endings[None], 0.0), axis=1)
    coef = jnp.where((places < place)[:, None], jnp.exp(exponent), 0.0)
    coef = jnp.repeat(coef, head_size, axis=1)
    skip = jnp.repeat(head_skip_weight, head_size)[None, :]

    result = None
    for group, (a, n) in enumerate(bounds):
        arrived = arrivals[group]
        if result is not None and group + 1 < len(bounds):
            arrived, result = lax.optimization_barrier((arrived, result))
        x, carried = states(order, arrived, inputs_t, factors, a, n, tile_cols)
        gathered = lax.all_gather(carried, "pos")
        result = outputs(
            result, x, scores, readout, cum, grow, source, gathered, coef, skip, a, n, tile_cols
        )
    return result[None]


def solution(mesh):
    in_specs = (
        P("stream", "pos", None),
        P("stream", "pos", None),
        P("stream", "pos", None),
        P(),
        P(),
        P(),
    )
    return jax.shard_map(
        on_device,
        mesh=mesh,
        in_specs=in_specs,
        out_specs=P("stream", "pos", None),
        check_vma=False,
    )
```

```python
import jax
import jax.numpy as jnp
from jax import lax
from jax.experimental import pallas as pl
from jax.experimental.pallas import tpu as pltpu
from jax.sharding import PartitionSpec as P

TILE_HEADS = 8
ROWS = 128
GROUPS = (6, 8, 2)
LOG2E = 1.4426950408889634
VMEM = 58 * 1024 * 1024


def expand(factors, pair, low):
    return jnp.where(low, factors[:, 2 * pair : 2 * pair + 1], factors[:, 2 * pair + 1 : 2 * pair + 2])


def state_kernel(order_ref, arrived_ref, inputs_t_ref, factor_ref, x_ref, carried_ref, scaled_ref):
    x = jnp.dot(order_ref[...], arrived_ref[...], preferred_element_type=jnp.float32)
    x_ref[...] = x.astype(jnp.bfloat16)
    factors = factor_ref[0]
    rows = x.shape[0]
    low = lax.broadcasted_iota(jnp.int32, (rows, 128), 1) < 64
    for pair in range(TILE_HEADS // 2):
        part = slice(128 * pair, 128 * pair + 128)
        scaled_ref[:, part] = (expand(factors, pair, low) * x[:, part]).astype(jnp.bfloat16)
    carried_ref[...] = jnp.dot(
        inputs_t_ref[...], scaled_ref[...], preferred_element_type=jnp.float32
    ).astype(jnp.bfloat16)


def output_kernel(
    x_ref,
    scores_ref,
    readout_ref,
    cum_ref,
    grow_ref,
    source_ref,
    carried_ref,
    coef_ref,
    skip_ref,
    *rest,
):
    out_ref, inherited_ref = rest[-2:]
    peers = carried_ref.shape[0]
    state = coef_ref[0:1, :] * carried_ref[0].astype(jnp.float32)
    for k in range(1, peers):
        state = state + coef_ref[k : k + 1, :] * carried_ref[k].astype(jnp.float32)
    inherited_ref[...] = jnp.dot(
        readout_ref[...], state.astype(jnp.bfloat16), preferred_element_type=jnp.float32
    )
    length = x_ref.shape[0]
    low = lax.broadcasted_iota(jnp.int32, (length, 128), 1) < 64
    low_rows = low[:ROWS]
    causal = lax.broadcasted_iota(jnp.int32, (ROWS, ROWS), 0) >= lax.broadcasted_iota(
        jnp.int32, (ROWS, ROWS), 1
    )
    cum = cum_ref[0]
    grow = grow_ref[0]
    source = source_ref[0]
    for pair in range(TILE_HEADS // 2):
        part = slice(128 * pair, 128 * pair + 128)
        x = x_ref[:, part]
        zero = jnp.zeros_like(x)
        halves = (jnp.where(low, x, zero), jnp.where(low, zero, x))
        for tile in range(length // ROWS):
            here = slice(ROWS * tile, ROWS * tile + ROWS)
            total = expand(grow[here], pair, low_rows) * inherited_ref[here, part]
            total = total + skip_ref[:, part] * x[here].astype(jnp.float32)
            for which in range(2):
                head = 2 * pair + which
                last = cum[here, head : head + 1]
                pieces = []
                if tile:
                    gap = last - source[head : head + 1, : ROWS * tile]
                    pieces.append(
                        (scores_ref[here, : ROWS * tile] * jnp.exp2(gap)).astype(jnp.bfloat16)
                    )
                gap = jnp.where(causal, last - source[head : head + 1, here], -jnp.inf)
                pieces.append((scores_ref[here, here] * jnp.exp2(gap)).astype(jnp.bfloat16))
                weights = pieces[0] if len(pieces) == 1 else jnp.concatenate(pieces, axis=1)
                total = total + jnp.dot(
                    weights,
                    halves[which][: ROWS * (tile + 1)],
                    preferred_element_type=jnp.float32,
                )
            out_ref[here, part] = total.astype(jnp.bfloat16)


def states(order, arrived, inputs_t, factors, first, tiles, tile_cols):
    rows, slots = order.shape
    state_size = inputs_t.shape[0]
    cols = tiles * tile_cols
    return pl.pallas_call(
        state_kernel,
        grid=(tiles,),
        in_specs=[
            pl.BlockSpec((rows, slots), lambda i: (0, 0)),
            pl.BlockSpec((slots, tile_cols), lambda i: (0, i)),
            pl.BlockSpec((state_size, rows), lambda i: (0, 0)),
            pl.BlockSpec((1, rows, TILE_HEADS), lambda i: (first + i, 0, 0)),
        ],
        out_specs=[
            pl.BlockSpec((rows, tile_cols), lambda i: (0, i)),
            pl.BlockSpec((state_size, tile_cols), lambda i: (0, i)),
        ],
        out_shape=[
            jax.ShapeDtypeStruct((rows, cols), jnp.bfloat16),
            jax.ShapeDtypeStruct((state_size, cols), jnp.bfloat16),
        ],
        scratch_shapes=[pltpu.VMEM((rows, tile_cols), jnp.bfloat16)],
        compiler_params=pltpu.CompilerParams(vmem_limit_bytes=VMEM),
        cost_estimate=pl.CostEstimate(
            flops=2 * rows * slots * cols + 2 * rows * state_size * cols,
            bytes_accessed=2 * (slots + rows + state_size) * cols,
            transcendentals=0,
        ),
    )(order, arrived, inputs_t, factors)


def outputs(previous, x, scores, readout, cum, grow, source, carried, coef, skip, first, tiles, tile_cols):
    rows = x.shape[0]
    state_size = readout.shape[1]
    peers = carried.shape[0]
    cols = tiles * tile_cols
    whole = coef.shape[1]
    in_specs = [
        pl.BlockSpec((rows, tile_cols), lambda i: (0, i)),
        pl.BlockSpec((rows, rows), lambda i: (0, 0)),
        pl.BlockSpec((rows, state_size), lambda i: (0, 0)),
        pl.BlockSpec((1, rows, TILE_HEADS), lambda i: (first + i, 0, 0)),
        pl.BlockSpec((1, rows, TILE_HEADS), lambda i: (first + i, 0, 0)),
        pl.BlockSpec((1, TILE_HEADS, rows), lambda i: (first + i, 0, 0)),
        pl.BlockSpec((peers, state_size, tile_cols), lambda i: (0, 0, i)),
        pl.BlockSpec((peers, tile_cols), lambda i: (0, first + i)),
        pl.BlockSpec((1, tile_cols), lambda i: (0, first + i)),
    ]
    operands = [x, scores, readout, cum, grow, source, carried, coef, skip]
    aliases = {}
    if previous is not None:
        in_specs.append(pl.BlockSpec(memory_space=pl.ANY))
        aliases = {len(operands): 0}
        operands.append(previous)
    return pl.pallas_call(
        output_kernel,
        grid=(tiles,),
        in_specs=in_specs,
        out_specs=pl.BlockSpec((rows, tile_cols), lambda i: (0, first + i)),
        out_shape=jax.ShapeDtypeStruct((rows, whole), jnp.bfloat16),
        scratch_shapes=[pltpu.VMEM((rows, tile_cols), jnp.float32)],
        input_output_aliases=aliases,
        compiler_params=pltpu.CompilerParams(vmem_limit_bytes=VMEM),
        cost_estimate=pl.CostEstimate(
            flops=2 * rows * (rows * 3 + state_size) * cols,
            bytes_accessed=2 * (2 * rows + peers * state_size) * cols,
            transcendentals=rows * rows * TILE_HEADS * tiles,
        ),
    )(*operands)


def on_device(tokens_in, proj_in, step_raw, decay_log, head_skip_weight, row_counts):
    streams = lax.axis_size("stream")
    stream = lax.axis_index("stream")
    place = lax.axis_index("pos")
    peers = lax.axis_size("pos")
    tokens = tokens_in[0]
    rows, inner = tokens.shape
    heads = step_raw.shape[2]
    head_size = inner // heads
    state_size = proj_in.shape[2] // 2
    capacity = 3 * rows // (2 * streams)
    slots = streams * capacity
    tile_cols = TILE_HEADS * head_size
    all_tiles = heads // TILE_HEADS

    counts = lax.dynamic_index_in_dim(row_counts, place, 0, keepdims=False)
    sent = lax.dynamic_index_in_dim(counts, stream, 0, keepdims=False)
    received = lax.dynamic_index_in_dim(counts, stream, 1, keepdims=False)
    send_start = jnp.cumsum(sent) - sent
    recv_start = jnp.cumsum(received) - received
    slot = jnp.arange(capacity, dtype=jnp.int32)
    picked = (send_start[:, None] + slot[None, :]).reshape(slots)
    position = jnp.arange(rows, dtype=jnp.int32)
    pack = (picked[:, None] == position[None, :]).astype(jnp.bfloat16)
    landed = jnp.where(
        slot[None, :] < received[:, None], recv_start[:, None] + slot[None, :], -1
    ).reshape(slots)
    order = (position[:, None] == landed[None, :]).astype(jnp.bfloat16)

    def packed(block):
        return jnp.dot(pack, block, preferred_element_type=jnp.bfloat16)

    def exchange(block):
        width = block.shape[1]
        block = block.reshape(streams, capacity, width)
        arrived = lax.all_to_all(block, "stream", split_axis=0, concat_axis=0, tiled=True)
        return arrived.reshape(slots, width)

    bounds = []
    first = 0
    for share in GROUPS:
        tiles = share * all_tiles // 16
        bounds.append((first, tiles))
        first += tiles

    def columns(group):
        a, n = bounds[group]
        return tokens[:, a * tile_cols : (a + n) * tile_cols]

    leading = packed(jnp.concatenate([columns(0), proj_in[0], step_raw[0]], axis=1))
    later = lax.optimization_barrier([packed(columns(g)) for g in range(1, len(bounds))])
    arrivals = [exchange(block) for block in [leading, *later]]
    ahead = bounds[0][1] * tile_cols
    small = jnp.dot(order, arrivals[0][:, ahead:], preferred_element_type=jnp.bfloat16)
    inputs = small[:, :state_size]
    readout = small[:, state_size : 2 * state_size]
    steps = jax.nn.softplus(small[:, 2 * state_size :].astype(jnp.float32))
    cumulated = jnp.cumsum(steps * -jnp.exp(decay_log)[None, :], axis=0)
    ending = cumulated[-1]
    scores = jnp.dot(readout, inputs.T, preferred_element_type=jnp.float32)
    inputs_t = inputs.T

    def by_tile(array):
        return jnp.moveaxis(array.reshape(rows, all_tiles, TILE_HEADS), 1, 0)

    factors = by_tile(jnp.exp(ending[None, :] - cumulated) * steps)
    grow = by_tile(jnp.exp(cumulated))
    cum = by_tile(cumulated * LOG2E)
    source = (cumulated * LOG2E - jnp.log2(steps)).T.reshape(all_tiles, TILE_HEADS, rows)

    endings = lax.all_gather(ending, "pos")
    places = jnp.arange(peers, dtype=jnp.int32)
    between = (places[None, :] > places[:, None]) & (places[None, :] < place)
    exponent = jnp.sum(jnp.where(between[:, :, None], endings[None], 0.0), axis=1)
    coef = jnp.where((places < place)[:, None], jnp.exp(exponent), 0.0)
    coef = jnp.repeat(coef, head_size, axis=1)
    skip = jnp.repeat(head_skip_weight, head_size)[None, :]

    result = None
    for group, (a, n) in enumerate(bounds):
        arrived = arrivals[group]
        if result is not None and group + 1 < len(bounds):
            arrived, result = lax.optimization_barrier((arrived, result))
        x, carried = states(order, arrived, inputs_t, factors, a, n, tile_cols)
        gathered = lax.all_gather(carried, "pos")
        result = outputs(
            result, x, scores, readout, cum, grow, source, gathered, coef, skip, a, n, tile_cols
        )
    return result[None]


def solution(mesh):
    in_specs = (
        P("stream", "pos", None),
        P("stream", "pos", None),
        P("stream", "pos", None),
        P(),
        P(),
        P(),
    )
    return jax.shard_map(
        on_device,
        mesh=mesh,
        in_specs=in_specs,
        out_specs=P("stream", "pos", None),
        check_vma=False,
    )
```
